32 devices in a mesh: groups: 2 (over y), adapter: 4 (over z), replica: 2 (over x), tp: 2 (over core).
Axes of the slice: x: 2, y: 2, z: 4, core: 2. Of those that a mesh axis runs over, the one named last changes fastest.
Arguments:
- tokens: bfloat16 [4, 256, 8192], P(('groups', 'replica'), 'adapter', 'tp'), parts along dimension 0, may hold values from -6 to 6
- token_adapter_index: int32 [4, 256, 1], P(('groups', 'replica')), parts along dimension 0, may hold values from 0 to 3; in each aligned block of 64 rows (0 to 63, 64 to 127, ..., all dimensions but the last counted through in order) at most 32 rows name the same one
- query_weight: bfloat16 [8192, 8192], P('tp', 'adapter'), may hold values from -0.0625 to 0.0625
- shrink_weight: bfloat16 [4, 8192, 64], P('adapter', 'tp'), may hold values from -0.0625 to 0.0625
- expand_weight: bfloat16 [4, 64, 8192], P('adapter'), may hold values from -0.75 to 0.75
Outputs:
- queries: bfloat16 [4, 256, 8192], P(('groups', 'replica'), ('adapter', 'tp')), parts along dimension 0
The draws below stay inside these ranges and needn't reach their ends.
There are 2 independent parts, one for each index of `groups`. The reference program is written for one: setup_inputs(seed, part) draws one part's arguments, and reference() takes and returns one part's arrays. A program takes and returns all parts, laid end to end along the dimension named above; an argument that names none is the same for every part. Nothing has to cross between parts.
Inputs may be any that keep to these rules, and one draw needn't show every extreme that they name: `token_adapter_index`: in each aligned block of 64 tokens of a replica (the tokens of one device), no adapter is named by more than 32 tokens, and in some blocks one adapter is named by exactly 32.
All inputs are finite; a program needn't handle non-finite values.
Results may differ from the reference program's by a relative error of at most 0.0054.
Values may be sent and summed in bfloat16 or wider, within the bound.
No kernel may reach another device: no remote copies, remote signals or barrier semaphores. Data moves between devices by JAX's collectives and lax.ppermute only.
A program may use at most 64 MiB of HBM per device.

```python
import math
import jax
import jax.numpy as jnp
import numpy as np
from jax import lax

MODEL_WIDTH = 8192
QUERY_FEATURES = 8192
ADAPTER_RANK = 64
TOK_DEV = 64
CAP = 32
ADAPTER_SLOTS = 4
TA = 256
N_REPLICA = 2


def levels(stream_key, extent, split, least, top_value):
    loudness = 1.0
    for axis_at, blocks in split:
        draws = jax.random.uniform(jax.random.fold_in(jax.random.fold_in(stream_key, 6), axis_at), (blocks,), jnp.float32, least / len(split), top_value / len(split))
        loudness = loudness * jnp.repeat(jnp.exp(draws), extent[axis_at] // blocks).reshape((-1,) + (1,) * (len(extent) - 1 - axis_at))
    return loudness


def shared_out(key, own, number, rows, number_of, top, limit, skew):
    order = jax.random.permutation(key, number_of)
    crowded, usual = portions_of(number_of, rows * top, limit, skew, True), portions_of(number_of, rows * top, limit, skew, False)
    places = jnp.arange(number_of)

    def named(lengths, offset_by):
        used = int((lengths > 0).sum())
        fixed = max(1, used // 4)
        moved = fixed + (places - fixed + offset_by * (used - fixed)) % max(1, number_of - fixed)
        return jnp.zeros((number_of,), jnp.int32).at[order[jnp.where(places < fixed, places, moved)]].set(jnp.asarray(lengths, jnp.int32))

    lengths = jnp.where(number % 4 == 0, named(crowded, number // 4), named(usual, number - number // 4 - 1))
    mixed = jax.random.permutation(jax.random.fold_in(own, 3), number_of)
    giver, sink = mixed[0:number_of // 2 * 2:2], mixed[1:number_of // 2 * 2:2]
    slack = jnp.minimum(lengths[giver] - 1, limit - lengths[sink]) // 2
    slack = jnp.where((giver == order[0]) | (sink == order[0]) | (lengths[sink] == 0), 0, jnp.maximum(slack, 0))
    moved = jax.random.randint(jax.random.fold_in(own, 4), (number_of // 2,), 0, 1 << 20) % (slack + 1)
    lengths = lengths.at[giver].add(-moved).at[sink].add(moved)
    labels = jnp.searchsorted(jnp.cumsum(lengths), jnp.arange(rows * top), side="right").astype(jnp.int32)
    grid = labels.reshape(top, rows).T
    grid = grid[jax.random.permutation(jax.random.fold_in(own, 1), rows)]
    offset_by = jax.random.randint(jax.random.fold_in(own, 2), (rows, 1), 0, top)
    return jnp.take_along_axis(grid, (jnp.arange(top)[None, :] + offset_by) % top, axis=1)


def portions_of(count, total, bound, skew, full):
    loads = [(1 << 20) // math.isqrt(grade ** skew) + 1 for grade in range(1, count + 1)]
    largest = bound if full else min(bound, max(-(-total // count), total * loads[0] // sum(loads)))
    least = 1 if total - largest >= count - 1 else 0
    given, spare = [largest] + [least] * (count - 1), total - largest - least * (count - 1)
    while spare > 0:
        movable = [i for i in range(1, count) if given[i] < largest] or [i for i in range(1, count) if given[i] < bound]
        whole, budget = sum([loads[i] for i in movable]), spare
        for i in movable:
            addition = min(bound - given[i], max(1, budget * loads[i] // whole), spare)
            given[i] = given[i] + addition
            spare = spare - addition
    return np.array(given)


def scatter_about(stream_key, shape, spread, bound, cuts=(), dtype=jnp.bfloat16):
    result = jax.random.normal(stream_key, shape, jnp.float32) * spread
    if len(cuts) > 0:
        result = levels(stream_key, shape, cuts, -0.22, 0.18) * result
    return jnp.clip(result, min=-bound, max=bound).astype(dtype)


def setup_inputs(seed: int = 0, part: int = 0) -> dict:
    arg_keys = jax.random.split(jax.random.key(seed), 6)
    part_keys = jax.random.split(jax.random.fold_in(arg_keys[5], part), 6)
    tokens = scatter_about(part_keys[0], (N_REPLICA, TA, MODEL_WIDTH), 1.0, 6.0, ((0, 2), (1, 4), (2, 2)))
    token_adapter_index_keys = jax.random.split(jax.random.fold_in(part_keys[1], 1), N_REPLICA * TA // TOK_DEV)
    token_adapter_index_turns = jax.random.permutation(jax.random.fold_in(part_keys[1], 3), N_REPLICA * TA // TOK_DEV)
    token_adapter_index = jax.vmap(lambda own, number: shared_out(jax.random.fold_in(part_keys[1], 2), own, number, TOK_DEV, ADAPTER_SLOTS, 1, CAP, 2))(token_adapter_index_keys, token_adapter_index_turns).reshape((N_REPLICA, TA, 1))
    query_weight = scatter_about(arg_keys[2], (MODEL_WIDTH, QUERY_FEATURES), MODEL_WIDTH ** -0.5, 0.0625, ((0, 2), (1, 4)))
    shrink_weight = scatter_about(arg_keys[3], (ADAPTER_SLOTS, MODEL_WIDTH, ADAPTER_RANK), MODEL_WIDTH ** -0.5, 0.0625, ((0, 4), (1, 2)))
    expand_weight = scatter_about(arg_keys[4], (ADAPTER_SLOTS, ADAPTER_RANK, QUERY_FEATURES), ADAPTER_RANK ** -0.5, 0.75, ((0, 4),))
    return {"tokens": tokens, "token_adapter_index": token_adapter_index, "query_weight": query_weight, "shrink_weight": shrink_weight, "expand_weight": expand_weight}


LOW_RANK_SCALE = 2.0


def reference(tokens, token_adapter_index, query_weight, shrink_weight, expand_weight):
    flat_rows = tokens.reshape(-1, MODEL_WIDTH)
    flat_ids = token_adapter_index.reshape(-1).astype(jnp.int32)
    base_output = jnp.dot(flat_rows, query_weight, preferred_element_type=jnp.float32)
    token_count = flat_rows.shape[0]
    block_rows = 64 if token_count % 64 == 0 else TOK_DEV

    def adapt_block(operands):
        xblock, block_index = operands
        shrink_matrix = shrink_weight[block_index].astype(jnp.float32)
        rank_activation = jnp.einsum("nd,ndr->nr", xblock.astype(jnp.float32), shrink_matrix).astype(jnp.bfloat16)
        expand_matrix = expand_weight[block_index].astype(jnp.float32)
        expanded = jnp.einsum("nr,nrk->nk", rank_activation.astype(jnp.float32), expand_matrix)
        return (LOW_RANK_SCALE * expanded).astype(jnp.bfloat16)

    delta_rows = lax.map(adapt_block, (flat_rows.reshape(-1, block_rows, MODEL_WIDTH), flat_ids.reshape(-1, block_rows)))
    low_rank_delta = delta_rows.reshape(token_count, QUERY_FEATURES)
    queries = (base_output + low_rank_delta.astype(jnp.float32)).astype(jnp.bfloat16)
    return queries.reshape(N_REPLICA, -1, QUERY_FEATURES)
```

```python
import jax
import jax.numpy as jnp
from jax import lax
from jax.experimental import pallas as pl
from jax.experimental.pallas import tpu as pltpu
from jax.sharding import PartitionSpec as P

LOW_RANK_SCALE = 2.0
F32 = jnp.float32
BF16 = jnp.bfloat16

FROM_NEXT = ((1, 0), (3, 1), (2, 3), (0, 2))
FROM_LAST = ((0, 1), (1, 3), (3, 2), (2, 0))
OPPOSITE = ((0, 3), (3, 0), (1, 2), (2, 1))
INNER = ((1, 2), (2, 1))
RELAY = ((2, 3), (1, 0))


def shift(x, pairs, axis="adapter"):
    return lax.ppermute(x, axis, pairs)


def swap(x, axis):
    return lax.ppermute(x, axis, ((0, 1), (1, 0)))


def both(x, axis, dim):
    other = swap(x, axis)
    first = lax.axis_index(axis) == 0
    return jnp.concatenate([jnp.where(first, x, other), jnp.where(first, other, x)], dim)


def after(x, *earlier):
    return lax.optimization_barrier((x,) + earlier)[0]


def place_kernel(where_ref, *refs):
    step = pl.program_id(0)
    for i, source in enumerate(refs[:-1]):

        @pl.when(step == i)
        def _(source=source):
            refs[-1][...] = source[...]


def place(where, blocks):
    rows, width = blocks[0].shape
    return pl.pallas_call(
        place_kernel,
        out_shape=jax.ShapeDtypeStruct((rows, len(blocks) * width), blocks[0].dtype),
        grid_spec=pltpu.PrefetchScalarGridSpec(
            num_scalar_prefetch=1,
            grid=(len(blocks),),
            in_specs=[pl.BlockSpec((rows, width), lambda i, where: (0, 0))] * len(blocks),
            out_specs=pl.BlockSpec((rows, width), lambda i, where: (0, where[i])),
        ),
    )(where, *blocks)


def dot(a, b):
    return jnp.dot(a, b, preferred_element_type=F32)


def gray(v):
    return v ^ (v >> 1)


def line_of_four(tokens, token_adapter_index, query_weight, shrink_weight, expand_weight):
    me = lax.axis_index("adapter")
    tp = lax.axis_index("tp")
    planes = [me] + [gray((gray(me) + i) % 4) for i in range(1, 4)]
    own = tokens[0]
    rows = own.shape[0]
    half = rows // 2
    width = query_weight.shape[1]
    shrink = shrink_weight[0]
    rank = shrink.shape[1]
    ids = token_adapter_index[0]

    def rank_of(x, i):
        named = lax.dynamic_slice_in_dim(ids, planes[i] * rows, rows) == me
        return jnp.where(named, dot(x, shrink), 0.0).astype(BF16)

    x1 = shift(own, FROM_NEXT)
    x3 = shift(own, FROM_LAST)
    x2a = shift(own, INNER)
    x2b = shift(x1, RELAY)

    peers = lax.axis_size("groups") * lax.axis_size("replica") * lax.axis_size("tp")
    peer = (lax.axis_index("groups") * lax.axis_size("replica") + lax.axis_index("replica")) * lax.axis_size("tp") + tp
    share = rank // peers
    r0 = rank_of(own, 0)
    part = lax.dynamic_slice_in_dim(after(expand_weight[0], x1), peer * share, share)

    def columns(i):
        return lax.dynamic_slice_in_dim(part, planes[i] * width, width, 1)

    panels = jnp.stack(
        [columns(0), shift(columns(3), FROM_NEXT), shift(columns(2), OPPOSITE), shift(columns(1), FROM_LAST)]
    )
    panels = both(both(both(panels, "tp", 1), "replica", 1), "groups", 1).reshape(4 * rank, width)

    base0 = dot(own, query_weight)
    r1 = rank_of(x1, 1)
    base1 = dot(x1, query_weight)
    x3, base0, base1 = lax.optimization_barrier((x3, base0, base1))
    r3 = rank_of(x3, 3)
    early = jnp.concatenate([r0, r1, r3])
    early = [early, shift(early, FROM_NEXT), shift(early, OPPOSITE), shift(early, FROM_LAST)]
    base3 = dot(x3, query_weight)
    x2a, x2b, base3 = lax.optimization_barrier((x2a, x2b, base3))
    x2 = jnp.where((me == 1) | (me == 2), x2a, x2b)
    r2 = rank_of(x2, 2)
    late = [r2, shift(r2, FROM_NEXT), shift(r2, OPPOSITE), shift(r2, FROM_LAST)]
    base2 = dot(x2, query_weight)
    base = [base0, base1, base2, base3]

    def rank_at(j, k):
        return late[j] if k == 2 else early[j][rows * (0, 1, None, 2)[k]:][:rows]

    wide = [jnp.concatenate([rank_at(j, (i - j) % 4) for j in range(4)], 1) for i in range(4)]

    def partial(side):
        at = side * half
        take = lambda x: lax.dynamic_slice_in_dim(x, at, half)
        ranks = jnp.concatenate([take(x) for x in wide])
        bases = jnp.concatenate([take(x) for x in base])
        return bases + LOW_RANK_SCALE * dot(ranks, panels)

    theirs = swap(partial(1 - tp).astype(BF16), "tp")
    full = (partial(tp) + theirs).astype(BF16).reshape(4, half, width)
    back = [full[0], shift(full[3], FROM_NEXT), shift(full[2], OPPOSITE), shift(full[1], FROM_LAST)]
    return place(jnp.stack(planes).astype(jnp.int32), back)[None]


def any_length(tokens, token_adapter_index, query_weight, shrink_weight, expand_weight):
    own_rows = tokens[0]
    tok_rows = own_rows.shape[0]
    features = own_rows.shape[1]
    neighbor_count = lax.axis_size("adapter")
    slot_capacity = max(2, 2 * tok_rows // neighbor_count)
    own_index = lax.axis_index("adapter")
    tp_index = lax.axis_index("tp")
    all_ids = token_adapter_index[0, :, 0]
    by_source = all_ids.reshape(neighbor_count, tok_rows)
    matches = (
        by_source[:, :, None] == jnp.arange(neighbor_count, dtype=jnp.int32)[None, None, :]
    ).astype(jnp.int32)
    order_in = jnp.sum((jnp.cumsum(matches, axis=1) - matches) * matches, axis=2)
    slot_index = by_source * slot_capacity + order_in
    send_slots = lax.dynamic_index_in_dim(slot_index, own_index, 0, keepdims=False)
    slot_range = jnp.arange(neighbor_count * slot_capacity, dtype=jnp.int32)
    partial_value = jnp.dot(
        lax.all_gather(own_rows, "adapter", axis=0, tiled=True),
        query_weight,
        preferred_element_type=jnp.float32,
    )
    packer = (slot_range[:, None] == send_slots[None, :]).astype(jnp.bfloat16)
    outgoing = jnp.dot(packer, own_rows, preferred_element_type=jnp.float32).astype(jnp.bfloat16)
    outgoing = outgoing.reshape(neighbor_count, slot_capacity, features)
    received_rows = lax.all_to_all(
        outgoing, "adapter", split_axis=0, concat_axis=0, tiled=True
    ).reshape(neighbor_count * slot_capacity, features)
    shrink_output = jnp.dot(received_rows, shrink_weight[0], preferred_element_type=jnp.float32)
    rank_activation = lax.psum(shrink_output, "tp").astype(jnp.bfloat16)
    half_rows = tok_rows // 2
    low_rank_delta = (
        LOW_RANK_SCALE
        * jnp.dot(rank_activation, expand_weight[0], preferred_element_type=jnp.float32)
    ).astype(jnp.bfloat16)
    returned = lax.all_to_all(
        low_rank_delta.reshape(neighbor_count, slot_capacity, -1),
        "adapter",
        split_axis=0,
        concat_axis=0,
        tiled=True,
    )
    returned = returned.reshape(neighbor_count * slot_capacity, -1)
    my_slots = lax.dynamic_slice_in_dim(send_slots, tp_index * half_rows, half_rows)
    placer = (my_slots[:, None] == slot_range[None, :]).astype(jnp.bfloat16)
    added = jnp.dot(placer, returned, preferred_element_type=jnp.float32)
    moved = lax.all_to_all(partial_value, "adapter", split_axis=0, concat_axis=1, tiled=True)
    home_rows = lax.psum_scatter(moved, "tp", scatter_dimension=0, tiled=True)
    queries = (home_rows + added).astype(jnp.bfloat16)
    return queries[None]


def solution(mesh):
    placed = (
        P(("groups", "replica"), "adapter", "tp"),
        P(("groups", "replica"), None, None),
        P("tp", "adapter"),
        P("adapter", "tp", None),
        P("adapter", None, None),
    )
    four = mesh.shape["adapter"] == 4 and all(mesh.shape[a] == 2 for a in ("groups", "replica", "tp"))
    return jax.shard_map(
        line_of_four if four else any_length,
        mesh=mesh,
        in_specs=placed,
        out_specs=P(("groups", "replica"), ("adapter", "tp"), None),
        check_vma=False,
    )
```

```python
import jax
import jax.numpy as jnp
from jax import lax
from jax.experimental import pallas as pl
from jax.experimental.pallas import tpu as pltpu
from jax.sharding import PartitionSpec as P

LOW_RANK_SCALE = 2.0
F32 = jnp.float32
BF16 = jnp.bfloat16
VMEM_LIMIT = 44 * 2**20

FROM_NEXT = ((1, 0), (3, 1), (2, 3), (0, 2))
FROM_LAST = ((0, 1), (1, 3), (3, 2), (2, 0))
OPPOSITE = ((0, 3), (3, 0), (1, 2), (2, 1))
INNER = ((1, 2), (2, 1))
RELAY = ((2, 3), (1, 0))


def shift(x, pairs, axis="adapter"):
    return lax.ppermute(x, axis, pairs)


def swap(x, axis):
    return lax.ppermute(x, axis, ((0, 1), (1, 0)))


def both(x, axis, dim):
    other = swap(x, axis)
    first = lax.axis_index(axis) == 0
    return jnp.concatenate([jnp.where(first, x, other), jnp.where(first, other, x)], dim)


def after(x, *earlier):
    return lax.optimization_barrier((x,) + earlier)[0]


def place_kernel(where_ref, *refs):
    width = refs[0].shape[1]
    for i, source in enumerate(refs[:-1]):
        refs[-1][:, pl.ds(pl.multiple_of(where_ref[i] * width, 128), width)] = source[...]


def place(where, blocks):
    rows, width = blocks[0].shape
    return pl.pallas_call(
        place_kernel,
        out_shape=jax.ShapeDtypeStruct((rows, len(blocks) * width), blocks[0].dtype),
        in_specs=[pl.BlockSpec(memory_space=pltpu.SMEM)] + [pl.BlockSpec(memory_space=pltpu.VMEM)] * len(blocks),
        out_specs=pl.BlockSpec(memory_space=pltpu.VMEM),
        compiler_params=pltpu.CompilerParams(vmem_limit_bytes=4 * 2**20),
    )(where, *blocks)


def base_kernel(inner_ref, *refs):
    *x_refs, weight_ref, out_ref, x_ref, held_ref, sems = refs
    count, depth, _ = held_ref.shape

    def part(k):
        return pltpu.make_async_copy(weight_ref.at[pl.ds(k * depth, depth)], held_ref.at[k], sems.at[k])

    for k in range(count):
        part(k).start()
    rows = x_refs[0].shape[0]
    for i, block in enumerate(x_refs):
        at = pl.ds(min(i, 2) * rows, rows)
        if i < 2:
            x_ref[at] = block[...]
        else:

            @pl.when(inner_ref[0] == 3 - i)
            def _(at=at, block=block):
                x_ref[at] = block[...]

    for k in range(count):
        part(k).wait()
        term = dot(x_ref[:, k * depth : (k + 1) * depth], held_ref[k])
        if k == 0:
            out_ref[...] = term
        else:
            out_ref[...] += term


def base_of(inner, blocks, weight):
    rows, depth = blocks[0].shape
    count = min(len(blocks), 3)
    width = weight.shape[1]
    parts = 8
    vmem = pl.BlockSpec(memory_space=pltpu.VMEM)
    return pl.pallas_call(
        base_kernel,
        out_shape=jax.ShapeDtypeStruct((count * rows, width), F32),
        in_specs=[pl.BlockSpec(memory_space=pltpu.SMEM)]
        + [vmem] * len(blocks)
        + [pl.BlockSpec(memory_space=pl.ANY)],
        out_specs=vmem,
        scratch_shapes=[
            pltpu.VMEM((count * rows, depth), weight.dtype),
            pltpu.VMEM((parts, depth // parts, width), weight.dtype),
            pltpu.SemaphoreType.DMA((parts,)),
        ],
        compiler_params=pltpu.CompilerParams(vmem_limit_bytes=VMEM_LIMIT),
        cost_estimate=pl.CostEstimate(
            flops=2 * count * rows * depth * width, bytes_accessed=weight.size * 2, transcendentals=0
        ),
    )(inner, *blocks, weight)


def dot(a, b):
    return jnp.dot(a, b, preferred_element_type=F32)


def gray(v):
    return v ^ (v >> 1)


def line_of_four(tokens, token_adapter_index, query_weight, shrink_weight, expand_weight):
    me = lax.axis_index("adapter")
    tp = lax.axis_index("tp")
    planes = [me] + [gray((gray(me) + i) % 4) for i in range(1, 4)]
    own = tokens[0]
    rows = own.shape[0]
    half = rows // 2
    width = query_weight.shape[1]
    shrink = shrink_weight[0]
    rank = shrink.shape[1]
    ids = token_adapter_index[0]

    x1 = shift(own, FROM_NEXT)
    inner = (me == 1) | (me == 2)
    base0 = base_of(jnp.ones((1,), jnp.int32), [own], query_weight)
    own, base0 = lax.optimization_barrier((own, base0))
    x3 = shift(own, FROM_LAST)
    x2a = shift(own, INNER)

    inside = ("replica", "tp")
    peers = lax.axis_size(inside)
    peer = lax.axis_index(inside)
    share = rank // peers
    part = lax.dynamic_slice_in_dim(after(expand_weight[0], base0), peer * share, share)

    def columns(i):
        return lax.dynamic_slice_in_dim(part, planes[i] * width, width, 1)

    part = jnp.stack(
        [columns(0), shift(columns(3), FROM_NEXT), shift(columns(2), OPPOSITE), shift(columns(1), FROM_LAST)]
    ).reshape(4 * share, width)
    x1, part = lax.optimization_barrier((x1, part))
    x2b = shift(x1, RELAY)
    x3, x2a, x2b = lax.optimization_barrier((x3, x2a, x2b))
    parts = [part] + [shift(part, [(i, i ^ k) for i in range(peers)], inside) for k in range(1, peers)]
    to = jnp.arange(4 * rank)[:, None]
    at = jnp.arange(4 * rank)[None, :]
    picked = at == ((to % rank // share) ^ peer) * (4 * share) + to // rank * share + to % share
    panels = dot(picked.astype(BF16), jnp.concatenate(parts)).astype(BF16)

    x2 = jnp.where(inner, x2a, x2b)
    ranks = []
    for i, x in enumerate((own, x1, x2, x3)):
        named = lax.dynamic_slice_in_dim(ids, planes[i] * rows, rows) == me
        ranks.append(jnp.where(named, dot(x, shrink), 0.0).astype(BF16))
    ranks = jnp.concatenate(ranks)
    ranks = [ranks, shift(ranks, FROM_NEXT), shift(ranks, OPPOSITE), shift(ranks, FROM_LAST)]
    base = base_of(inner.astype(jnp.int32)[None], [x1, x3, x2a, x2b], query_weight)
    base = [base0, base[:rows], base[2 * rows :], base[rows : 2 * rows]]

    def rank_at(j, k):
        return ranks[j][k * rows:][:rows]

    wide = [jnp.concatenate([rank_at(j, (i - j) % 4) for j in range(4)], 1) for i in range(4)]

    def partial(side):
        at = side * half
        take = lambda x: lax.dynamic_slice_in_dim(x, at, half)
        ranks = jnp.concatenate([take(x) for x in wide])
        bases = jnp.concatenate([take(x) for x in base])
        return bases + LOW_RANK_SCALE * dot(ranks, panels)

    theirs = swap(partial(1 - tp).astype(BF16), "tp")
    full = (partial(tp) + theirs).astype(BF16).reshape(4, half, width)
    back = [full[0], shift(full[3], FROM_NEXT), shift(full[2], OPPOSITE), shift(full[1], FROM_LAST)]
    return place(jnp.stack(planes).astype(jnp.int32), back)[None]


def any_length(tokens, token_adapter_index, query_weight, shrink_weight, expand_weight):
    own_rows = tokens[0]
    tok_rows = own_rows.shape[0]
    features = own_rows.shape[1]
    neighbor_count = lax.axis_size("adapter")
    slot_capacity = max(2, 2 * tok_rows // neighbor_count)
    own_index = lax.axis_index("adapter")
    tp_index = lax.axis_index("tp")
    all_ids = token_adapter_index[0, :, 0]
    by_source = all_ids.reshape(neighbor_count, tok_rows)
    matches = (
        by_source[:, :, None] == jnp.arange(neighbor_count, dtype=jnp.int32)[None, None, :]
    ).astype(jnp.int32)
    order_in = jnp.sum((jnp.cumsum(matches, axis=1) - matches) * matches, axis=2)
    slot_index = by_source * slot_capacity + order_in
    send_slots = lax.dynamic_index_in_dim(slot_index, own_index, 0, keepdims=False)
    slot_range = jnp.arange(neighbor_count * slot_capacity, dtype=jnp.int32)
    partial_value = jnp.dot(
        lax.all_gather(own_rows, "adapter", axis=0, tiled=True),
        query_weight,
        preferred_element_type=jnp.float32,
    )
    packer = (slot_range[:, None] == send_slots[None, :]).astype(jnp.bfloat16)
    outgoing = jnp.dot(packer, own_rows, preferred_element_type=jnp.float32).astype(jnp.bfloat16)
    outgoing = outgoing.reshape(neighbor_count, slot_capacity, features)
    received_rows = lax.all_to_all(
        outgoing, "adapter", split_axis=0, concat_axis=0, tiled=True
    ).reshape(neighbor_count * slot_capacity, features)
    shrink_output = jnp.dot(received_rows, shrink_weight[0], preferred_element_type=jnp.float32)
    rank_activation = lax.psum(shrink_output, "tp").astype(jnp.bfloat16)
    half_rows = tok_rows // 2
    low_rank_delta = (
        LOW_RANK_SCALE
        * jnp.dot(rank_activation, expand_weight[0], preferred_element_type=jnp.float32)
    ).astype(jnp.bfloat16)
    returned = lax.all_to_all(
        low_rank_delta.reshape(neighbor_count, slot_capacity, -1),
        "adapter",
        split_axis=0,
        concat_axis=0,
        tiled=True,
    )
    returned = returned.reshape(neighbor_count * slot_capacity, -1)
    my_slots = lax.dynamic_slice_in_dim(send_slots, tp_index * half_rows, half_rows)
    placer = (my_slots[:, None] == slot_range[None, :]).astype(jnp.bfloat16)
    added = jnp.dot(placer, returned, preferred_element_type=jnp.float32)
    moved = lax.all_to_all(partial_value, "adapter", split_axis=0, concat_axis=1, tiled=True)
    home_rows = lax.psum_scatter(moved, "tp", scatter_dimension=0, tiled=True)
    queries = (home_rows + added).astype(jnp.bfloat16)
    return queries[None]


def solution(mesh):
    placed = (
        P(("groups", "replica"), "adapter", "tp"),
        P(("groups", "replica"), None, None),
        P("tp", "adapter"),
        P("adapter", "tp", None),
        P("adapter", None, None),
    )
    four = mesh.shape["adapter"] == 4 and all(mesh.shape[a] == 2 for a in ("groups", "replica", "tp"))
    return jax.shard_map(
        line_of_four if four else any_length,
        mesh=mesh,
        in_specs=placed,
        out_specs=P(("groups", "replica"), ("adapter", "tp"), None),
        check_vma=False,
    )
```

```python
import functools

import jax
import jax.numpy as jnp
from jax import lax
from jax.experimental import pallas as pl
from jax.experimental.pallas import tpu as pltpu
from jax.sharding import PartitionSpec as P

LOW_RANK_SCALE = 2.0
F32 = jnp.float32
BF16 = jnp.bfloat16
VMEM_LIMIT = 44 * 2**20

FROM_NEXT = ((1, 0), (3, 1), (2, 3), (0, 2))
FROM_LAST = ((0, 1), (1, 3), (3, 2), (2, 0))
OPPOSITE = ((0, 3), (3, 0), (1, 2), (2, 1))
INNER = ((1, 2), (2, 1))
RELAY = ((2, 3), (1, 0))


def shift(x, pairs, axis="adapter"):
    return lax.ppermute(x, axis, pairs)


def swap(x, axis):
    return lax.ppermute(x, axis, ((0, 1), (1, 0)))


def both(x, axis, dim):
    other = swap(x, axis)
    first = lax.axis_index(axis) == 0
    return jnp.concatenate([jnp.where(first, x, other), jnp.where(first, other, x)], dim)


def after(x, *earlier):
    return lax.optimization_barrier((x,) + earlier)[0]


def place_kernel(where_ref, *refs):
    width = refs[0].shape[1]
    for i, source in enumerate(refs[:-1]):
        refs[-1][:, pl.ds(pl.multiple_of(where_ref[i] * width, 128), width)] = source[...]


def place(where, blocks):
    rows, width = blocks[0].shape
    return pl.pallas_call(
        place_kernel,
        out_shape=jax.ShapeDtypeStruct((rows, len(blocks) * width), blocks[0].dtype),
        in_specs=[pl.BlockSpec(memory_space=pltpu.SMEM)] + [pl.BlockSpec(memory_space=pltpu.VMEM)] * len(blocks),
        out_specs=pl.BlockSpec(memory_space=pltpu.VMEM),
        compiler_params=pltpu.CompilerParams(vmem_limit_bytes=4 * 2**20),
    )(where, *blocks)


def base_kernel(inner_ref, *refs, blocks, parts):
    x_refs, part_refs, weight_ref = refs[:blocks], refs[blocks : blocks + parts], refs[blocks + parts]
    out_ref, *panel_refs, x_ref, held_ref, sems = refs[blocks + parts + 1 :]
    count, depth, _ = held_ref.shape

    def piece(k):
        return pltpu.make_async_copy(weight_ref.at[pl.ds(k * depth, depth)], held_ref.at[k], sems.at[k])

    for k in range(count):
        piece(k).start()
    rows = x_refs[0].shape[0]
    for i, block in enumerate(x_refs):
        at = pl.ds(min(i, 2) * rows, rows)
        if i < 2:
            x_ref[at] = block[...]
        else:

            @pl.when(inner_ref[0] == 3 - i)
            def _(at=at, block=block):
                x_ref[at] = block[...]

    for k, part_ref in enumerate(part_refs):
        share = part_ref.shape[0] // 8
        for slot in range(4):
            first = part_ref[slot * share : (slot + 1) * share]
            second = part_ref[(4 + slot) * share : (5 + slot) * share]
            at = pl.multiple_of((slot * parts + (inner_ref[1] ^ k)) * 2 * share, 16)

            @pl.when(inner_ref[2] == 0)
            def _(at=at, first=first, second=second):
                panel_refs[0][pl.ds(at, 2 * share)] = jnp.concatenate([first, second])

            @pl.when(inner_ref[2] == 1)
            def _(at=at, first=first, second=second):
                panel_refs[0][pl.ds(at, 2 * share)] = jnp.concatenate([second, first])

    for k in range(count):
        piece(k).wait()
        term = dot(x_ref[:, k * depth : (k + 1) * depth], held_ref[k])
        if k == 0:
            out_ref[...] = term
        else:
            out_ref[...] += term


def base_of(facts, blocks, parts, weight):
    rows, depth = blocks[0].shape
    count = min(len(blocks), 3)
    width = weight.shape[1]
    pieces = 8
    vmem = pl.BlockSpec(memory_space=pltpu.VMEM)
    shapes = [jax.ShapeDtypeStruct((count * rows, width), F32)]
    if parts:
        shapes.append(jax.ShapeDtypeStruct((len(parts) * parts[0].shape[0], width), parts[0].dtype))
    return pl.pallas_call(
        functools.partial(base_kernel, blocks=len(blocks), parts=len(parts)),
        out_shape=shapes,
        in_specs=[pl.BlockSpec(memory_space=pltpu.SMEM)]
        + [vmem] * (len(blocks) + len(parts))
        + [pl.BlockSpec(memory_space=pl.ANY)],
        out_specs=[vmem] * len(shapes),
        scratch_shapes=[
            pltpu.VMEM((count * rows, depth), weight.dtype),
            pltpu.VMEM((pieces, depth // pieces, width), weight.dtype),
            pltpu.SemaphoreType.DMA((pieces,)),
        ],
        compiler_params=pltpu.CompilerParams(vmem_limit_bytes=VMEM_LIMIT),
        cost_estimate=pl.CostEstimate(
            flops=2 * count * rows * depth * width, bytes_accessed=weight.size * 2, transcendentals=0
        ),
    )(facts, *blocks, *parts, weight)


def dot(a, b):
    return jnp.dot(a, b, preferred_element_type=F32)


def gray(v):
    return v ^ (v >> 1)


def line_of_four(tokens, token_adapter_index, query_weight, shrink_weight, expand_weight):
    me = lax.axis_index("adapter")
    tp = lax.axis_index("tp")
    planes = [me] + [gray((gray(me) + i) % 4) for i in range(1, 4)]
    own = tokens[0]
    rows = own.shape[0]
    half = rows // 2
    width = query_weight.shape[1]
    shrink = shrink_weight[0]
    rank = shrink.shape[1]
    ids = token_adapter_index[0]

    x1 = shift(own, FROM_NEXT)
    inner = (me == 1) | (me == 2)
    [base0] = base_of(jnp.ones((3,), jnp.int32), [own], [], query_weight)
    own, base0 = lax.optimization_barrier((own, base0))
    x3 = shift(own, FROM_LAST)
    x2a = shift(own, INNER)

    inside = ("replica", "tp")
    peers = lax.axis_size(inside)
    peer = lax.axis_index(inside)
    group = lax.axis_index("groups")
    share = rank // peers // 2
    part = lax.dynamic_slice_in_dim(after(expand_weight[0], base0), (peer * 2 + group) * share, share)

    def columns(i):
        return lax.dynamic_slice_in_dim(part, planes[i] * width, width, 1)

    part = jnp.stack(
        [columns(0), shift(columns(3), FROM_NEXT), shift(columns(2), OPPOSITE), shift(columns(1), FROM_LAST)]
    )
    x1, part = lax.optimization_barrier((x1, part))
    x2b = shift(x1, RELAY)
    x3, x2a, x2b = lax.optimization_barrier((x3, x2a, x2b))
    part = jnp.concatenate([part.reshape(4 * share, width), swap(part, "groups").reshape(4 * share, width)])
    parts = [part] + [shift(part, [(i, i ^ k) for i in range(peers)], inside) for k in range(1, peers)]

    x2 = jnp.where(inner, x2a, x2b)
    ranks = []
    for i, x in enumerate((own, x1, x2, x3)):
        named = lax.dynamic_slice_in_dim(ids, planes[i] * rows, rows) == me
        ranks.append(jnp.where(named, dot(x, shrink), 0.0).astype(BF16))
    ranks = jnp.concatenate(ranks)
    ranks = [ranks, shift(ranks, FROM_NEXT), shift(ranks, OPPOSITE), shift(ranks, FROM_LAST)]
    facts = jnp.stack([inner.astype(jnp.int32), peer.astype(jnp.int32), group.astype(jnp.int32)])
    base, panels = base_of(facts, [x1, x3, x2a, x2b], parts, query_weight)
    base = [base0, base[:rows], base[2 * rows :], base[rows : 2 * rows]]

    def rank_at(j, k):
        return ranks[j][k * rows:][:rows]

    wide = [jnp.concatenate([rank_at(j, (i - j) % 4) for j in range(4)], 1) for i in range(4)]

    def partial(side):
        at = side * half
        take = lambda x: lax.dynamic_slice_in_dim(x, at, half)
        ranks = jnp.concatenate([take(x) for x in wide])
        bases = jnp.concatenate([take(x) for x in base])
        return bases + LOW_RANK_SCALE * dot(ranks, panels)

    theirs = swap(partial(1 - tp).astype(BF16), "tp")
    full = (partial(tp) + theirs).astype(BF16).reshape(4, half, width)
    back = [full[0], shift(full[3], FROM_NEXT), shift(full[2], OPPOSITE), shift(full[1], FROM_LAST)]
    return place(jnp.stack(planes).astype(jnp.int32), back)[None]


def any_length(tokens, token_adapter_index, query_weight, shrink_weight, expand_weight):
    own_rows = tokens[0]
    tok_rows = own_rows.shape[0]
    features = own_rows.shape[1]
    neighbor_count = lax.axis_size("adapter")
    slot_capacity = max(2, 2 * tok_rows // neighbor_count)
    own_index = lax.axis_index("adapter")
    tp_index = lax.axis_index("tp")
    all_ids = token_adapter_index[0, :, 0]
    by_source = all_ids.reshape(neighbor_count, tok_rows)
    matches = (
        by_source[:, :, None] == jnp.arange(neighbor_count, dtype=jnp.int32)[None, None, :]
    ).astype(jnp.int32)
    order_in = jnp.sum((jnp.cumsum(matches, axis=1) - matches) * matches, axis=2)
    slot_index = by_source * slot_capacity + order_in
    send_slots = lax.dynamic_index_in_dim(slot_index, own_index, 0, keepdims=False)
    slot_range = jnp.arange(neighbor_count * slot_capacity, dtype=jnp.int32)
    partial_value = jnp.dot(
        lax.all_gather(own_rows, "adapter", axis=0, tiled=True),
        query_weight,
        preferred_element_type=jnp.float32,
    )
    packer = (slot_range[:, None] == send_slots[None, :]).astype(jnp.bfloat16)
    outgoing = jnp.dot(packer, own_rows, preferred_element_type=jnp.float32).astype(jnp.bfloat16)
    outgoing = outgoing.reshape(neighbor_count, slot_capacity, features)
    received_rows = lax.all_to_all(
        outgoing, "adapter", split_axis=0, concat_axis=0, tiled=True
    ).reshape(neighbor_count * slot_capacity, features)
    shrink_output = jnp.dot(received_rows, shrink_weight[0], preferred_element_type=jnp.float32)
    rank_activation = lax.psum(shrink_output, "tp").astype(jnp.bfloat16)
    half_rows = tok_rows // 2
    low_rank_delta = (
        LOW_RANK_SCALE
        * jnp.dot(rank_activation, expand_weight[0], preferred_element_type=jnp.float32)
    ).astype(jnp.bfloat16)
    returned = lax.all_to_all(
        low_rank_delta.reshape(neighbor_count, slot_capacity, -1),
        "adapter",
        split_axis=0,
        concat_axis=0,
        tiled=True,
    )
    returned = returned.reshape(neighbor_count * slot_capacity, -1)
    my_slots = lax.dynamic_slice_in_dim(send_slots, tp_index * half_rows, half_rows)
    placer = (my_slots[:, None] == slot_range[None, :]).astype(jnp.bfloat16)
    added = jnp.dot(placer, returned, preferred_element_type=jnp.float32)
    moved = lax.all_to_all(partial_value, "adapter", split_axis=0, concat_axis=1, tiled=True)
    home_rows = lax.psum_scatter(moved, "tp", scatter_dimension=0, tiled=True)
    queries = (home_rows + added).astype(jnp.bfloat16)
    return queries[None]


def solution(mesh):
    placed = (
        P(("groups", "replica"), "adapter", "tp"),
        P(("groups", "replica"), None, None),
        P("tp", "adapter"),
        P("adapter", "tp", None),
        P("adapter", None, None),
    )
    four = mesh.shape["adapter"] == 4 and all(mesh.shape[a] == 2 for a in ("groups", "replica", "tp"))
    return jax.shard_map(
        line_of_four if four else any_length,
        mesh=mesh,
        in_specs=placed,
        out_specs=P(("groups", "replica"), ("adapter", "tp"), None),
        check_vma=False,
    )
```

```python
import jax
import jax.numpy as jnp
from jax import lax
from jax.experimental import pallas as pl
from jax.experimental.pallas import tpu as pltpu
from jax.sharding import PartitionSpec as P

LOW_RANK_SCALE = 2.0
F32 = jnp.float32
BF16 = jnp.bfloat16
FIRST_LIMIT = 44 * 2**20
NEXT_LIMIT = 20 * 2**20
LAST_LIMIT = 12 * 2**20

FROM_NEXT = ((1, 0), (3, 1), (2, 3), (0, 2))
FROM_LAST = ((0, 1), (1, 3), (3, 2), (2, 0))
OPPOSITE = ((0, 3), (3, 0), (1, 2), (2, 1))
INNER = ((1, 2), (2, 1))
RELAY = ((2, 3), (1, 0))


def shift(x, pairs, axis="adapter"):
    return lax.ppermute(x, axis, pairs)


def swap(x, axis):
    return lax.ppermute(x, axis, ((0, 1), (1, 0)))


def both(x, axis, dim):
    other = swap(x, axis)
    first = lax.axis_index(axis) == 0
    return jnp.concatenate([jnp.where(first, x, other), jnp.where(first, other, x)], dim)


def after(x, *earlier):
    return lax.optimization_barrier((x,) + earlier)[0]


def place_kernel(where_ref, *refs):
    width = refs[0].shape[1]
    for i, source in enumerate(refs[:-1]):
        refs[-1][:, pl.ds(pl.multiple_of(where_ref[i] * width, 128), width)] = source[...]


def place(where, blocks):
    rows, width = blocks[0].shape
    return pl.pallas_call(
        place_kernel,
        out_shape=jax.ShapeDtypeStruct((rows, len(blocks) * width), blocks[0].dtype),
        in_specs=[pl.BlockSpec(memory_space=pltpu.SMEM)] + [pl.BlockSpec(memory_space=pltpu.VMEM)] * len(blocks),
        out_specs=pl.BlockSpec(memory_space=pltpu.VMEM),
        compiler_params=pltpu.CompilerParams(vmem_limit_bytes=4 * 2**20),
    )(where, *blocks)


VMEM = pl.BlockSpec(memory_space=pltpu.VMEM)
SMEM = pl.BlockSpec(memory_space=pltpu.SMEM)


def cost(rows, weight):
    return pl.CostEstimate(flops=2 * rows * weight.size, bytes_accessed=weight.size * 2, transcendentals=0)


def stream_kernel(x_ref, weight_ref, out_ref, held_ref, sems):
    count, depth, _ = held_ref.shape

    def piece(k):
        return pltpu.make_async_copy(weight_ref.at[pl.ds(k * depth, depth)], held_ref.at[k], sems.at[k])

    for k in range(count):
        piece(k).start()
    for k in range(count):
        piece(k).wait()
        term = dot(x_ref[:, k * depth : (k + 1) * depth], held_ref[k])
        if k == 0:
            out_ref[...] = term
        else:
            out_ref[...] += term


def stream(x, weight, limit):
    rows, depth = x.shape
    width = weight.shape[1]
    pieces = 8
    return pl.pallas_call(
        stream_kernel,
        out_shape=jax.ShapeDtypeStruct((rows, width), F32),
        in_specs=[VMEM, pl.BlockSpec(memory_space=pl.ANY)],
        out_specs=VMEM,
        scratch_shapes=[
            pltpu.VMEM((pieces, depth // pieces, width), weight.dtype),
            pltpu.SemaphoreType.DMA((pieces,)),
        ],
        compiler_params=pltpu.CompilerParams(vmem_limit_bytes=limit),
        cost_estimate=cost(rows, weight),
    )(x, weight)


def last_kernel(facts_ref, x3_ref, x2a_ref, x2b_ref, *refs):
    part_refs, (weight_ref, out_ref, panel_ref, x_ref) = refs[:-4], refs[-4:]
    rows = x3_ref.shape[0]
    x_ref[rows:] = x3_ref[...]

    @pl.when(facts_ref[0] == 1)
    def _():
        x_ref[:rows] = x2a_ref[...]

    @pl.when(facts_ref[0] == 0)
    def _():
        x_ref[:rows] = x2b_ref[...]

    for k, part_ref in enumerate(part_refs):
        share = part_ref.shape[0] // 8
        for slot in range(4):
            first = part_ref[slot * share : (slot + 1) * share]
            second = part_ref[(4 + slot) * share : (5 + slot) * share]
            at = pl.multiple_of((slot * len(part_refs) + (facts_ref[1] ^ k)) * 2 * share, 16)

            @pl.when(facts_ref[2] == 0)
            def _(at=at, first=first, second=second):
                panel_ref[pl.ds(at, 2 * share)] = jnp.concatenate([first, second])

            @pl.when(facts_ref[2] == 1)
            def _(at=at, first=first, second=second):
                panel_ref[pl.ds(at, 2 * share)] = jnp.concatenate([second, first])

    tile = 256

    @pl.loop(0, out_ref.shape[1] // tile)
    def _(n):
        at = pl.ds(pl.multiple_of(n * tile, tile), tile)
        out_ref[:, at] = dot(x_ref[...], weight_ref[:, at])


def last(facts, x3, x2a, x2b, parts, weight):
    rows, depth = x3.shape
    width = weight.shape[1]
    return pl.pallas_call(
        last_kernel,
        out_shape=[
            jax.ShapeDtypeStruct((2 * rows, width), F32),
            jax.ShapeDtypeStruct((len(parts) * parts[0].shape[0], width), parts[0].dtype),
        ],
        in_specs=[SMEM] + [VMEM] * (4 + len(parts)),
        out_specs=[VMEM, VMEM],
        scratch_shapes=[pltpu.VMEM((2 * rows, depth), weight.dtype)],
        compiler_params=pltpu.CompilerParams(vmem_limit_bytes=LAST_LIMIT),
        cost_estimate=cost(2 * rows, weight),
    )(facts, x3, x2a, x2b, *parts, weight)


def dot(a, b):
    return jnp.dot(a, b, preferred_element_type=F32)


def gray(v):
    return v ^ (v >> 1)


def line_of_four(tokens, token_adapter_index, query_weight, shrink_weight, expand_weight):
    me = lax.axis_index("adapter")
    tp = lax.axis_index("tp")
    planes = [me] + [gray((gray(me) + i) % 4) for i in range(1, 4)]
    own = tokens[0]
    rows = own.shape[0]
    half = rows // 2
    width = query_weight.shape[1]
    shrink = shrink_weight[0]
    rank = shrink.shape[1]
    ids = token_adapter_index[0]

    x1 = shift(own, FROM_NEXT)
    inner = (me == 1) | (me == 2)
    base0 = stream(own, query_weight, FIRST_LIMIT)
    own, base0 = lax.optimization_barrier((own, base0))
    x3 = shift(own, FROM_LAST)
    x2a = shift(own, INNER)

    inside = ("replica", "tp")
    peers = lax.axis_size(inside)
    peer = lax.axis_index(inside)
    group = lax.axis_index("groups")
    share = rank // peers // 2
    part = lax.dynamic_slice_in_dim(after(expand_weight[0], base0), (peer * 2 + group) * share, share)

    def columns(i):
        return lax.dynamic_slice_in_dim(part, planes[i] * width, width, 1)

    part = jnp.stack(
        [columns(0), shift(columns(3), FROM_NEXT), shift(columns(2), OPPOSITE), shift(columns(1), FROM_LAST)]
    )
    x1, part = lax.optimization_barrier((x1, part))
    x2b = shift(x1, RELAY)
    base1 = stream(x1, query_weight, NEXT_LIMIT)
    x3, x2a, x2b, base1 = lax.optimization_barrier((x3, x2a, x2b, base1))
    part = jnp.concatenate([part.reshape(4 * share, width), swap(part, "groups").reshape(4 * share, width)])
    parts = [part] + [shift(part, [(i, i ^ k) for i in range(peers)], inside) for k in range(1, peers)]

    x2 = jnp.where(inner, x2a, x2b)
    ranks = []
    for i, x in enumerate((own, x1, x2, x3)):
        named = lax.dynamic_slice_in_dim(ids, planes[i] * rows, rows) == me
        ranks.append(jnp.where(named, dot(x, shrink), 0.0).astype(BF16))
    ranks = jnp.concatenate(ranks)
    ranks = [ranks, shift(ranks, FROM_NEXT), shift(ranks, OPPOSITE), shift(ranks, FROM_LAST)]
    facts = jnp.stack([inner.astype(jnp.int32), peer.astype(jnp.int32), group.astype(jnp.int32)])
    base23, panels = last(facts, x3, x2a, x2b, parts, query_weight)
    base = [base0, base1, base23[:rows], base23[rows:]]

    def rank_at(j, k):
        return ranks[j][k * rows:][:rows]

    wide = [jnp.concatenate([rank_at(j, (i - j) % 4) for j in range(4)], 1) for i in range(4)]

    def partial(side):
        at = side * half
        take = lambda x: lax.dynamic_slice_in_dim(x, at, half)
        ranks = jnp.concatenate([take(x) for x in wide])
        bases = jnp.concatenate([take(x) for x in base])
        return bases + LOW_RANK_SCALE * dot(ranks, panels)

    theirs = swap(partial(1 - tp).astype(BF16), "tp")
    full = (partial(tp) + theirs).astype(BF16).reshape(4, half, width)
    back = [full[0], shift(full[3], FROM_NEXT), shift(full[2], OPPOSITE), shift(full[1], FROM_LAST)]
    return place(jnp.stack(planes).astype(jnp.int32), back)[None]


def any_length(tokens, token_adapter_index, query_weight, shrink_weight, expand_weight):
    own_rows = tokens[0]
    tok_rows = own_rows.shape[0]
    features = own_rows.shape[1]
    neighbor_count = lax.axis_size("adapter")
    slot_capacity = max(2, 2 * tok_rows // neighbor_count)
    own_index = lax.axis_index("adapter")
    tp_index = lax.axis_index("tp")
    all_ids = token_adapter_index[0, :, 0]
    by_source = all_ids.reshape(neighbor_count, tok_rows)
    matches = (
        by_source[:, :, None] == jnp.arange(neighbor_count, dtype=jnp.int32)[None, None, :]
    ).astype(jnp.int32)
    order_in = jnp.sum((jnp.cumsum(matches, axis=1) - matches) * matches, axis=2)
    slot_index = by_source * slot_capacity + order_in
    send_slots = lax.dynamic_index_in_dim(slot_index, own_index, 0, keepdims=False)
    slot_range = jnp.arange(neighbor_count * slot_capacity, dtype=jnp.int32)
    partial_value = jnp.dot(
        lax.all_gather(own_rows, "adapter", axis=0, tiled=True),
        query_weight,
        preferred_element_type=jnp.float32,
    )
    packer = (slot_range[:, None] == send_slots[None, :]).astype(jnp.bfloat16)
    outgoing = jnp.dot(packer, own_rows, preferred_element_type=jnp.float32).astype(jnp.bfloat16)
    outgoing = outgoing.reshape(neighbor_count, slot_capacity, features)
    received_rows = lax.all_to_all(
        outgoing, "adapter", split_axis=0, concat_axis=0, tiled=True
    ).reshape(neighbor_count * slot_capacity, features)
    shrink_output = jnp.dot(received_rows, shrink_weight[0], preferred_element_type=jnp.float32)
    rank_activation = lax.psum(shrink_output, "tp").astype(jnp.bfloat16)
    half_rows = tok_rows // 2
    low_rank_delta = (
        LOW_RANK_SCALE
        * jnp.dot(rank_activation, expand_weight[0], preferred_element_type=jnp.float32)
    ).astype(jnp.bfloat16)
    returned = lax.all_to_all(
        low_rank_delta.reshape(neighbor_count, slot_capacity, -1),
        "adapter",
        split_axis=0,
        concat_axis=0,
        tiled=True,
    )
    returned = returned.reshape(neighbor_count * slot_capacity, -1)
    my_slots = lax.dynamic_slice_in_dim(send_slots, tp_index * half_rows, half_rows)
    placer = (my_slots[:, None] == slot_range[None, :]).astype(jnp.bfloat16)
    added = jnp.dot(placer, returned, preferred_element_type=jnp.float32)
    moved = lax.all_to_all(partial_value, "adapter", split_axis=0, concat_axis=1, tiled=True)
    home_rows = lax.psum_scatter(moved, "tp", scatter_dimension=0, tiled=True)
    queries = (home_rows + added).astype(jnp.bfloat16)
    return queries[None]


def solution(mesh):
    placed = (
        P(("groups", "replica"), "adapter", "tp"),
        P(("groups", "replica"), None, None),
        P("tp", "adapter"),
        P("adapter", "tp", None),
        P("adapter", None, None),
    )
    four = mesh.shape["adapter"] == 4 and all(mesh.shape[a] == 2 for a in ("groups", "replica", "tp"))
    return jax.shard_map(
        line_of_four if four else any_length,
        mesh=mesh,
        in_specs=placed,
        out_specs=P(("groups", "replica"), ("adapter", "tp"), None),
        check_vma=False,
    )
```

```python
import jax
import jax.numpy as jnp
from jax import lax
from jax.experimental import pallas as pl
from jax.experimental.pallas import tpu as pltpu
from jax.sharding import PartitionSpec as P

LOW_RANK_SCALE = 2.0
F32 = jnp.float32
BF16 = jnp.bfloat16
FIRST_LIMIT = 44 * 2**20
NEXT_LIMIT = 20 * 2**20
LAST_LIMIT = 12 * 2**20

FROM_NEXT = ((1, 0), (3, 1), (2, 3), (0, 2))
FROM_LAST = ((0, 1), (1, 3), (3, 2), (2, 0))
OPPOSITE = ((0, 3), (3, 0), (1, 2), (2, 1))
INNER = ((1, 2), (2, 1))
RELAY = ((2, 3), (1, 0))


def shift(x, pairs, axis="adapter"):
    return lax.ppermute(x, axis, pairs)


def swap(x, axis):
    return lax.ppermute(x, axis, ((0, 1), (1, 0)))


def both(x, axis, dim):
    other = swap(x, axis)
    first = lax.axis_index(axis) == 0
    return jnp.concatenate([jnp.where(first, x, other), jnp.where(first, other, x)], dim)


def after(x, *earlier):
    return lax.optimization_barrier((x,) + earlier)[0]


def place_kernel(where_ref, *refs):
    width = refs[0].shape[1]
    for i, source in enumerate(refs[:-1]):
        refs[-1][:, pl.ds(pl.multiple_of(where_ref[i] * width, 128), width)] = source[...]


def place(where, blocks):
    rows, width = blocks[0].shape
    return pl.pallas_call(
        place_kernel,
        out_shape=jax.ShapeDtypeStruct((rows, len(blocks) * width), blocks[0].dtype),
        in_specs=[pl.BlockSpec(memory_space=pltpu.SMEM)] + [pl.BlockSpec(memory_space=pltpu.VMEM)] * len(blocks),
        out_specs=pl.BlockSpec(memory_space=pltpu.VMEM),
        compiler_params=pltpu.CompilerParams(vmem_limit_bytes=4 * 2**20),
    )(where, *blocks)


VMEM = pl.BlockSpec(memory_space=pltpu.VMEM)
SMEM = pl.BlockSpec(memory_space=pltpu.SMEM)


def cost(rows, weight):
    return pl.CostEstimate(flops=2 * rows * weight.size, bytes_accessed=weight.size * 2, transcendentals=0)


def stream_kernel(x_ref, weight_ref, out_ref, held_ref, sems):
    count, depth, _ = held_ref.shape

    def piece(k):
        return pltpu.make_async_copy(weight_ref.at[pl.ds(k * depth, depth)], held_ref.at[k], sems.at[k])

    for k in range(count):
        piece(k).start()
    for k in range(count):
        piece(k).wait()
        term = dot(x_ref[:, k * depth : (k + 1) * depth], held_ref[k])
        if k == 0:
            out_ref[...] = term
        else:
            out_ref[...] += term


def stream(x, weight, limit):
    rows, depth = x.shape
    width = weight.shape[1]
    pieces = 8
    return pl.pallas_call(
        stream_kernel,
        out_shape=jax.ShapeDtypeStruct((rows, width), F32),
        in_specs=[VMEM, pl.BlockSpec(memory_space=pl.ANY)],
        out_specs=VMEM,
        scratch_shapes=[
            pltpu.VMEM((pieces, depth // pieces, width), weight.dtype),
            pltpu.SemaphoreType.DMA((pieces,)),
        ],
        compiler_params=pltpu.CompilerParams(vmem_limit_bytes=limit),
        cost_estimate=cost(rows, weight),
    )(x, weight)


def last_kernel(facts_ref, x3_ref, x2a_ref, x2b_ref, *refs):
    part_refs, (weight_ref, out_ref, panel_ref, x_ref) = refs[:-4], refs[-4:]
    rows = x3_ref.shape[0]
    x_ref[rows:] = x3_ref[...]

    @pl.when(facts_ref[0] == 1)
    def _():
        x_ref[:rows] = x2a_ref[...]

    @pl.when(facts_ref[0] == 0)
    def _():
        x_ref[:rows] = x2b_ref[...]

    for k, part_ref in enumerate(part_refs):
        share = part_ref.shape[0] // 8
        for slot in range(4):
            first = part_ref[slot * share : (slot + 1) * share]
            second = part_ref[(4 + slot) * share : (5 + slot) * share]
            at = pl.multiple_of((slot * len(part_refs) + (facts_ref[1] ^ k)) * 2 * share, 16)

            @pl.when(facts_ref[2] == 0)
            def _(at=at, first=first, second=second):
                panel_ref[pl.ds(at, 2 * share)] = jnp.concatenate([first, second])

            @pl.when(facts_ref[2] == 1)
            def _(at=at, first=first, second=second):
                panel_ref[pl.ds(at, 2 * share)] = jnp.concatenate([second, first])

    tile = 256

    @pl.loop(0, out_ref.shape[1] // tile)
    def _(n):
        at = pl.ds(pl.multiple_of(n * tile, tile), tile)
        out_ref[:, at] = dot(x_ref[...], weight_ref[:, at])


def last(facts, x3, x2a, x2b, parts, weight):
    rows, depth = x3.shape
    width = weight.shape[1]
    return pl.pallas_call(
        last_kernel,
        out_shape=[
            jax.ShapeDtypeStruct((2 * rows, width), F32),
            jax.ShapeDtypeStruct((len(parts) * parts[0].shape[0], width), parts[0].dtype),
        ],
        in_specs=[SMEM] + [VMEM] * (4 + len(parts)),
        out_specs=[VMEM, VMEM],
        scratch_shapes=[pltpu.VMEM((2 * rows, depth), weight.dtype)],
        compiler_params=pltpu.CompilerParams(vmem_limit_bytes=LAST_LIMIT),
        cost_estimate=cost(2 * rows, weight),
    )(facts, x3, x2a, x2b, *parts, weight)


def dot(a, b):
    return jnp.dot(a, b, preferred_element_type=F32)


def gray(v):
    return v ^ (v >> 1)


def line_of_four(tokens, token_adapter_index, query_weight, shrink_weight, expand_weight):
    me = lax.axis_index("adapter")
    tp = lax.axis_index("tp")
    planes = [me] + [gray((gray(me) + i) % 4) for i in range(1, 4)]
    own = tokens[0]
    rows = own.shape[0]
    half = rows // 2
    width = query_weight.shape[1]
    shrink = shrink_weight[0]
    rank = shrink.shape[1]
    ids = token_adapter_index[0]

    x1 = shift(own, FROM_NEXT)
    inner = (me == 1) | (me == 2)
    base0 = stream(own, query_weight, FIRST_LIMIT)
    own, base0 = lax.optimization_barrier((own, base0))
    x3 = shift(own, FROM_LAST)

    inside = ("replica", "tp")
    peers = lax.axis_size(inside)
    peer = lax.axis_index(inside)
    group = lax.axis_index("groups")
    share = rank // peers // 2
    part = lax.dynamic_slice_in_dim(after(expand_weight[0], base0), (peer * 2 + group) * share, share)

    def columns(i):
        return lax.dynamic_slice_in_dim(part, planes[i] * width, width, 1)

    part = jnp.stack(
        [columns(0), shift(columns(3), FROM_NEXT), shift(columns(2), OPPOSITE), shift(columns(1), FROM_LAST)]
    )
    x1, part, own = lax.optimization_barrier((x1, part, own))
    x2a = shift(own, INNER)
    x2b = shift(x1, RELAY)
    base1 = stream(x1, query_weight, NEXT_LIMIT)
    x3, x2a, x2b, base1 = lax.optimization_barrier((x3, x2a, x2b, base1))
    part = jnp.concatenate([part.reshape(4 * share, width), swap(part, "groups").reshape(4 * share, width)])
    parts = [part] + [shift(part, [(i, i ^ k) for i in range(peers)], inside) for k in range(1, peers)]

    x2 = jnp.where(inner, x2a, x2b)
    ranks = []
    for i, x in enumerate((own, x1, x2, x3)):
        named = lax.dynamic_slice_in_dim(ids, planes[i] * rows, rows) == me
        ranks.append(jnp.where(named, dot(x, shrink), 0.0).astype(BF16))
    ranks = jnp.concatenate(ranks)
    ranks = [ranks, shift(ranks, FROM_NEXT), shift(ranks, OPPOSITE), shift(ranks, FROM_LAST)]
    facts = jnp.stack([inner.astype(jnp.int32), peer.astype(jnp.int32), group.astype(jnp.int32)])
    base23, panels = last(facts, x3, x2a, x2b, parts, query_weight)
    base = [base0, base1, base23[:rows], base23[rows:]]

    def rank_at(j, k):
        return ranks[j][k * rows:][:rows]

    wide = [jnp.concatenate([rank_at(j, (i - j) % 4) for j in range(4)], 1) for i in range(4)]

    def partial(side):
        at = side * half
        take = lambda x: lax.dynamic_slice_in_dim(x, at, half)
        ranks = jnp.concatenate([take(x) for x in wide])
        bases = jnp.concatenate([take(x) for x in base])
        return bases + LOW_RANK_SCALE * dot(ranks, panels)

    theirs = swap(partial(1 - tp).astype(BF16), "tp")
    full = (partial(tp) + theirs).astype(BF16).reshape(4, half, width)
    back = [full[0], shift(full[3], FROM_NEXT), shift(full[2], OPPOSITE), shift(full[1], FROM_LAST)]
    return place(jnp.stack(planes).astype(jnp.int32), back)[None]


def any_length(tokens, token_adapter_index, query_weight, shrink_weight, expand_weight):
    own_rows = tokens[0]
    tok_rows = own_rows.shape[0]
    features = own_rows.shape[1]
    neighbor_count = lax.axis_size("adapter")
    slot_capacity = max(2, 2 * tok_rows // neighbor_count)
    own_index = lax.axis_index("adapter")
    tp_index = lax.axis_index("tp")
    all_ids = token_adapter_index[0, :, 0]
    by_source = all_ids.reshape(neighbor_count, tok_rows)
    matches = (
        by_source[:, :, None] == jnp.arange(neighbor_count, dtype=jnp.int32)[None, None, :]
    ).astype(jnp.int32)
    order_in = jnp.sum((jnp.cumsum(matches, axis=1) - matches) * matches, axis=2)
    slot_index = by_source * slot_capacity + order_in
    send_slots = lax.dynamic_index_in_dim(slot_index, own_index, 0, keepdims=False)
    slot_range = jnp.arange(neighbor_count * slot_capacity, dtype=jnp.int32)
    partial_value = jnp.dot(
        lax.all_gather(own_rows, "adapter", axis=0, tiled=True),
        query_weight,
        preferred_element_type=jnp.float32,
    )
    packer = (slot_range[:, None] == send_slots[None, :]).astype(jnp.bfloat16)
    outgoing = jnp.dot(packer, own_rows, preferred_element_type=jnp.float32).astype(jnp.bfloat16)
    outgoing = outgoing.reshape(neighbor_count, slot_capacity, features)
    received_rows = lax.all_to_all(
        outgoing, "adapter", split_axis=0, concat_axis=0, tiled=True
    ).reshape(neighbor_count * slot_capacity, features)
    shrink_output = jnp.dot(received_rows, shrink_weight[0], preferred_element_type=jnp.float32)
    rank_activation = lax.psum(shrink_output, "tp").astype(jnp.bfloat16)
    half_rows = tok_rows // 2
    low_rank_delta = (
        LOW_RANK_SCALE
        * jnp.dot(rank_activation, expand_weight[0], preferred_element_type=jnp.float32)
    ).astype(jnp.bfloat16)
    returned = lax.all_to_all(
        low_rank_delta.reshape(neighbor_count, slot_capacity, -1),
        "adapter",
        split_axis=0,
        concat_axis=0,
        tiled=True,
    )
    returned = returned.reshape(neighbor_count * slot_capacity, -1)
    my_slots = lax.dynamic_slice_in_dim(send_slots, tp_index * half_rows, half_rows)
    placer = (my_slots[:, None] == slot_range[None, :]).astype(jnp.bfloat16)
    added = jnp.dot(placer, returned, preferred_element_type=jnp.float32)
    moved = lax.all_to_all(partial_value, "adapter", split_axis=0, concat_axis=1, tiled=True)
    home_rows = lax.psum_scatter(moved, "tp", scatter_dimension=0, tiled=True)
    queries = (home_rows + added).astype(jnp.bfloat16)
    return queries[None]


def solution(mesh):
    placed = (
        P(("groups", "replica"), "adapter", "tp"),
        P(("groups", "replica"), None, None),
        P("tp", "adapter"),
        P("adapter", "tp", None),
        P("adapter", None, None),
    )
    four = mesh.shape["adapter"] == 4 and all(mesh.shape[a] == 2 for a in ("groups", "replica", "tp"))
    return jax.shard_map(
        line_of_four if four else any_length,
        mesh=mesh,
        in_specs=placed,
        out_specs=P(("groups", "replica"), ("adapter", "tp"), None),
        check_vma=False,
    )
```

```python
import jax
import jax.numpy as jnp
from jax import lax
from jax.experimental import pallas as pl
from jax.experimental.pallas import tpu as pltpu
from jax.sharding import PartitionSpec as P

LOW_RANK_SCALE = 2.0
F32 = jnp.float32
BF16 = jnp.bfloat16
FIRST_LIMIT = 44 * 2**20
NEXT_LIMIT = 20 * 2**20
LAST_LIMIT = 12 * 2**20

FROM_NEXT = ((1, 0), (3, 1), (2, 3), (0, 2))
FROM_LAST = ((0, 1), (1, 3), (3, 2), (2, 0))
OPPOSITE = ((0, 3), (3, 0), (1, 2), (2, 1))
INNER = ((1, 2), (2, 1))
RELAY = ((2, 3), (1, 0))


def shift(x, pairs, axis="adapter"):
    return lax.ppermute(x, axis, pairs)


def swap(x, axis):
    return lax.ppermute(x, axis, ((0, 1), (1, 0)))


def both(x, axis, dim):
    other = swap(x, axis)
    first = lax.axis_index(axis) == 0
    return jnp.concatenate([jnp.where(first, x, other), jnp.where(first, other, x)], dim)


def after(x, *earlier):
    return lax.optimization_barrier((x,) + earlier)[0]


def place_kernel(where_ref, *refs):
    width = refs[0].shape[1]
    for i, source in enumerate(refs[:-1]):
        refs[-1][:, pl.ds(pl.multiple_of(where_ref[i] * width, 128), width)] = source[...]


def place(where, blocks):
    rows, width = blocks[0].shape
    return pl.pallas_call(
        place_kernel,
        out_shape=jax.ShapeDtypeStruct((rows, len(blocks) * width), blocks[0].dtype),
        in_specs=[pl.BlockSpec(memory_space=pltpu.SMEM)] + [pl.BlockSpec(memory_space=pltpu.VMEM)] * len(blocks),
        out_specs=pl.BlockSpec(memory_space=pltpu.VMEM),
        compiler_params=pltpu.CompilerParams(vmem_limit_bytes=4 * 2**20),
    )(where, *blocks)


VMEM = pl.BlockSpec(memory_space=pltpu.VMEM)
SMEM = pl.BlockSpec(memory_space=pltpu.SMEM)


def cost(rows, weight):
    return pl.CostEstimate(flops=2 * rows * weight.size, bytes_accessed=weight.size * 2, transcendentals=0)


def stream_kernel(x_ref, weight_ref, out_ref, held_ref, sems):
    count, depth, _ = held_ref.shape

    def piece(k):
        return pltpu.make_async_copy(weight_ref.at[pl.ds(k * depth, depth)], held_ref.at[k], sems.at[k])

    for k in range(count):
        piece(k).start()
    for k in range(count):
        piece(k).wait()
        term = dot(x_ref[:, k * depth : (k + 1) * depth], held_ref[k])
        if k == 0:
            out_ref[...] = term
        else:
            out_ref[...] += term


def stream(x, weight, limit):
    rows, depth = x.shape
    width = weight.shape[1]
    pieces = 8
    return pl.pallas_call(
        stream_kernel,
        out_shape=jax.ShapeDtypeStruct((rows, width), F32),
        in_specs=[VMEM, pl.BlockSpec(memory_space=pl.ANY)],
        out_specs=VMEM,
        scratch_shapes=[
            pltpu.VMEM((pieces, depth // pieces, width), weight.dtype),
            pltpu.SemaphoreType.DMA((pieces,)),
        ],
        compiler_params=pltpu.CompilerParams(vmem_limit_bytes=limit),
        cost_estimate=cost(rows, weight),
    )(x, weight)


def last_kernel(facts_ref, x3_ref, x2a_ref, x2b_ref, *refs):
    part_refs, (weight_ref, out_ref, panel_ref, x_ref) = refs[:-4], refs[-4:]
    rows = x3_ref.shape[0]
    x_ref[rows:] = x3_ref[...]

    @pl.when(facts_ref[0] == 1)
    def _():
        x_ref[:rows] = x2a_ref[...]

    @pl.when(facts_ref[0] == 0)
    def _():
        x_ref[:rows] = x2b_ref[...]

    for k, part_ref in enumerate(part_refs):
        share = part_ref.shape[0] // 8
        for slot in range(4):
            first = part_ref[slot * share : (slot + 1) * share]
            second = part_ref[(4 + slot) * share : (5 + slot) * share]
            at = pl.multiple_of((slot * len(part_refs) + (facts_ref[1] ^ k)) * 2 * share, 16)

            @pl.when(facts_ref[2] == 0)
            def _(at=at, first=first, second=second):
                panel_ref[pl.ds(at, 2 * share)] = jnp.concatenate([first, second])

            @pl.when(facts_ref[2] == 1)
            def _(at=at, first=first, second=second):
                panel_ref[pl.ds(at, 2 * share)] = jnp.concatenate([second, first])

    tile = 256

    @pl.loop(0, out_ref.shape[1] // tile)
    def _(n):
        at = pl.ds(pl.multiple_of(n * tile, tile), tile)
        out_ref[:, at] = dot(x_ref[...], weight_ref[:, at])


def last(facts, x3, x2a, x2b, parts, weight):
    rows, depth = x3.shape
    width = weight.shape[1]
    return pl.pallas_call(
        last_kernel,
        out_shape=[
            jax.ShapeDtypeStruct((2 * rows, width), F32),
            jax.ShapeDtypeStruct((len(parts) * parts[0].shape[0], width), parts[0].dtype),
        ],
        in_specs=[SMEM] + [VMEM] * (4 + len(parts)),
        out_specs=[VMEM, VMEM],
        scratch_shapes=[pltpu.VMEM((2 * rows, depth), weight.dtype)],
        compiler_params=pltpu.CompilerParams(vmem_limit_bytes=LAST_LIMIT),
        cost_estimate=cost(2 * rows, weight),
    )(facts, x3, x2a, x2b, *parts, weight)


def dot(a, b):
    return jnp.dot(a, b, preferred_element_type=F32)


def gray(v):
    return v ^ (v >> 1)


def line_of_four(tokens, token_adapter_index, query_weight, shrink_weight, expand_weight):
    me = lax.axis_index("adapter")
    tp = lax.axis_index("tp")
    planes = [me] + [gray((gray(me) + i) % 4) for i in range(1, 4)]
    own = tokens[0]
    rows = own.shape[0]
    half = rows // 2
    width = query_weight.shape[1]
    shrink = shrink_weight[0]
    rank = shrink.shape[1]
    ids = token_adapter_index[0]

    x1 = shift(own, FROM_NEXT)
    inner = (me == 1) | (me == 2)
    base0 = stream(own, query_weight, FIRST_LIMIT)
    own, base0 = lax.optimization_barrier((own, base0))
    x3 = shift(own, FROM_LAST)

    inside = ("replica", "tp")
    peers = lax.axis_size(inside)
    peer = lax.axis_index(inside)
    group = lax.axis_index("groups")
    share = rank // peers // 2
    part = lax.dynamic_slice_in_dim(after(expand_weight[0], base0), (peer * 2 + group) * share, share)

    def columns(i):
        return lax.dynamic_slice_in_dim(part, planes[i] * width, width, 1)

    part = jnp.stack(
        [columns(0), shift(columns(3), FROM_NEXT), shift(columns(2), OPPOSITE), shift(columns(1), FROM_LAST)]
    )
    x1, part, own = lax.optimization_barrier((x1, part, own))
    x2a = shift(own, INNER)
    x2b = shift(x1, RELAY)
    part = jnp.concatenate([part.reshape(4 * share, width), swap(part, "groups").reshape(4 * share, width)])
    base1 = stream(after(x1, part), query_weight, NEXT_LIMIT)
    parts = [part] + [shift(part, [(i, i ^ k) for i in range(peers)], inside) for k in range(1, peers)]
    x3, x2a, x2b, base1 = lax.optimization_barrier((x3, x2a, x2b, base1))

    x2 = jnp.where(inner, x2a, x2b)
    ranks = []
    for i, x in enumerate((own, x1, x2, x3)):
        named = lax.dynamic_slice_in_dim(ids, planes[i] * rows, rows) == me
        ranks.append(jnp.where(named, dot(x, shrink), 0.0).astype(BF16))
    ranks = jnp.concatenate(ranks)
    ranks = [ranks, shift(ranks, FROM_NEXT), shift(ranks, OPPOSITE), shift(ranks, FROM_LAST)]
    facts = jnp.stack([inner.astype(jnp.int32), peer.astype(jnp.int32), group.astype(jnp.int32)])
    base23, panels = last(facts, x3, x2a, x2b, parts, query_weight)
    base = [base0, base1, base23[:rows], base23[rows:]]

    def rank_at(j, k):
        return ranks[j][k * rows:][:rows]

    wide = [jnp.concatenate([rank_at(j, (i - j) % 4) for j in range(4)], 1) for i in range(4)]

    def partial(side):
        at = side * half
        take = lambda x: lax.dynamic_slice_in_dim(x, at, half)
        ranks = jnp.concatenate([take(x) for x in wide])
        bases = jnp.concatenate([take(x) for x in base])
        return bases + LOW_RANK_SCALE * dot(ranks, panels)

    theirs = swap(partial(1 - tp).astype(BF16), "tp")
    full = (partial(tp) + theirs).astype(BF16).reshape(4, half, width)
    back = [full[0], shift(full[3], FROM_NEXT), shift(full[2], OPPOSITE), shift(full[1], FROM_LAST)]
    return place(jnp.stack(planes).astype(jnp.int32), back)[None]


def any_length(tokens, token_adapter_index, query_weight, shrink_weight, expand_weight):
    own_rows = tokens[0]
    tok_rows = own_rows.shape[0]
    features = own_rows.shape[1]
    neighbor_count = lax.axis_size("adapter")
    slot_capacity = max(2, 2 * tok_rows // neighbor_count)
    own_index = lax.axis_index("adapter")
    tp_index = lax.axis_index("tp")
    all_ids = token_adapter_index[0, :, 0]
    by_source = all_ids.reshape(neighbor_count, tok_rows)
    matches = (
        by_source[:, :, None] == jnp.arange(neighbor_count, dtype=jnp.int32)[None, None, :]
    ).astype(jnp.int32)
    order_in = jnp.sum((jnp.cumsum(matches, axis=1) - matches) * matches, axis=2)
    slot_index = by_source * slot_capacity + order_in
    send_slots = lax.dynamic_index_in_dim(slot_index, own_index, 0, keepdims=False)
    slot_range = jnp.arange(neighbor_count * slot_capacity, dtype=jnp.int32)
    partial_value = jnp.dot(
        lax.all_gather(own_rows, "adapter", axis=0, tiled=True),
        query_weight,
        preferred_element_type=jnp.float32,
    )
    packer = (slot_range[:, None] == send_slots[None, :]).astype(jnp.bfloat16)
    outgoing = jnp.dot(packer, own_rows, preferred_element_type=jnp.float32).astype(jnp.bfloat16)
    outgoing = outgoing.reshape(neighbor_count, slot_capacity, features)
    received_rows = lax.all_to_all(
        outgoing, "adapter", split_axis=0, concat_axis=0, tiled=True
    ).reshape(neighbor_count * slot_capacity, features)
    shrink_output = jnp.dot(received_rows, shrink_weight[0], preferred_element_type=jnp.float32)
    rank_activation = lax.psum(shrink_output, "tp").astype(jnp.bfloat16)
    half_rows = tok_rows // 2
    low_rank_delta = (
        LOW_RANK_SCALE
        * jnp.dot(rank_activation, expand_weight[0], preferred_element_type=jnp.float32)
    ).astype(jnp.bfloat16)
    returned = lax.all_to_all(
        low_rank_delta.reshape(neighbor_count, slot_capacity, -1),
        "adapter",
        split_axis=0,
        concat_axis=0,
        tiled=True,
    )
    returned = returned.reshape(neighbor_count * slot_capacity, -1)
    my_slots = lax.dynamic_slice_in_dim(send_slots, tp_index * half_rows, half_rows)
    placer = (my_slots[:, None] == slot_range[None, :]).astype(jnp.bfloat16)
    added = jnp.dot(placer, returned, preferred_element_type=jnp.float32)
    moved = lax.all_to_all(partial_value, "adapter", split_axis=0, concat_axis=1, tiled=True)
    home_rows = lax.psum_scatter(moved, "tp", scatter_dimension=0, tiled=True)
    queries = (home_rows + added).astype(jnp.bfloat16)
    return queries[None]


def solution(mesh):
    placed = (
        P(("groups", "replica"), "adapter", "tp"),
        P(("groups", "replica"), None, None),
        P("tp", "adapter"),
        P("adapter", "tp", None),
        P("adapter", None, None),
    )
    four = mesh.shape["adapter"] == 4 and all(mesh.shape[a] == 2 for a in ("groups", "replica", "tp"))
    return jax.shard_map(
        line_of_four if four else any_length,
        mesh=mesh,
        in_specs=placed,
        out_specs=P(("groups", "replica"), ("adapter", "tp"), None),
        check_vma=False,
    )
```

```python
import jax
import jax.numpy as jnp
from jax import lax
from jax.experimental import pallas as pl
from jax.experimental.pallas import tpu as pltpu
from jax.sharding import PartitionSpec as P

LOW_RANK_SCALE = 2.0
F32 = jnp.float32
BF16 = jnp.bfloat16
FIRST_LIMIT = 44 * 2**20
NEXT_LIMIT = 20 * 2**20
LAST_LIMIT = 12 * 2**20

FROM_NEXT = ((1, 0), (3, 1), (2, 3), (0, 2))
FROM_LAST = ((0, 1), (1, 3), (3, 2), (2, 0))
OPPOSITE = ((0, 3), (3, 0), (1, 2), (2, 1))
INNER = ((1, 2), (2, 1))
RELAY = ((2, 3), (1, 0))


def shift(x, pairs, axis="adapter"):
    return lax.ppermute(x, axis, pairs)


def swap(x, axis):
    return lax.ppermute(x, axis, ((0, 1), (1, 0)))


def both(x, axis, dim):
    other = swap(x, axis)
    first = lax.axis_index(axis) == 0
    return jnp.concatenate([jnp.where(first, x, other), jnp.where(first, other, x)], dim)


def after(x, *earlier):
    return lax.optimization_barrier((x,) + earlier)[0]


def place_kernel(where_ref, *refs):
    width = refs[0].shape[1]
    for i, source in enumerate(refs[:-1]):
        refs[-1][:, pl.ds(pl.multiple_of(where_ref[i] * width, 128), width)] = source[...]


def place(where, blocks):
    rows, width = blocks[0].shape
    return pl.pallas_call(
        place_kernel,
        out_shape=jax.ShapeDtypeStruct((rows, len(blocks) * width), blocks[0].dtype),
        in_specs=[pl.BlockSpec(memory_space=pltpu.SMEM)] + [pl.BlockSpec(memory_space=pltpu.VMEM)] * len(blocks),
        out_specs=pl.BlockSpec(memory_space=pltpu.VMEM),
        compiler_params=pltpu.CompilerParams(vmem_limit_bytes=4 * 2**20),
    )(where, *blocks)


VMEM = pl.BlockSpec(memory_space=pltpu.VMEM)
SMEM = pl.BlockSpec(memory_space=pltpu.SMEM)


def cost(rows, weight):
    return pl.CostEstimate(flops=2 * rows * weight.size, bytes_accessed=weight.size * 2, transcendentals=0)


def stream_kernel(x_ref, weight_ref, out_ref, held_ref, sems):
    count, depth, _ = held_ref.shape

    def piece(k):
        return pltpu.make_async_copy(weight_ref.at[pl.ds(k * depth, depth)], held_ref.at[k], sems.at[k])

    for k in range(count):
        piece(k).start()
    for k in range(count):
        piece(k).wait()
        term = dot(x_ref[:, k * depth : (k + 1) * depth], held_ref[k])
        if k == 0:
            out_ref[...] = term
        else:
            out_ref[...] += term


def stream(x, weight, limit):
    rows, depth = x.shape
    width = weight.shape[1]
    pieces = 8
    return pl.pallas_call(
        stream_kernel,
        out_shape=jax.ShapeDtypeStruct((rows, width), F32),
        in_specs=[VMEM, pl.BlockSpec(memory_space=pl.ANY)],
        out_specs=VMEM,
        scratch_shapes=[
            pltpu.VMEM((pieces, depth // pieces, width), weight.dtype),
            pltpu.SemaphoreType.DMA((pieces,)),
        ],
        compiler_params=pltpu.CompilerParams(vmem_limit_bytes=limit),
        cost_estimate=cost(rows, weight),
    )(x, weight)


def last_kernel(facts_ref, x3_ref, x2a_ref, x2b_ref, *refs):
    part_refs, (weight_ref, out_ref, panel_ref, x_ref) = refs[:-4], refs[-4:]
    rows = x3_ref.shape[0]
    x_ref[rows:] = x3_ref[...]

    @pl.when(facts_ref[0] == 1)
    def _():
        x_ref[:rows] = x2a_ref[...]

    @pl.when(facts_ref[0] == 0)
    def _():
        x_ref[:rows] = x2b_ref[...]

    for k, part_ref in enumerate(part_refs):
        share = part_ref.shape[0] // 8
        for slot in range(4):
            first = part_ref[slot * share : (slot + 1) * share]
            second = part_ref[(4 + slot) * share : (5 + slot) * share]
            at = pl.multiple_of((slot * len(part_refs) + (facts_ref[1] ^ k)) * 2 * share, 16)

            @pl.when(facts_ref[2] == 0)
            def _(at=at, first=first, second=second):
                panel_ref[pl.ds(at, 2 * share)] = jnp.concatenate([first, second])

            @pl.when(facts_ref[2] == 1)
            def _(at=at, first=first, second=second):
                panel_ref[pl.ds(at, 2 * share)] = jnp.concatenate([second, first])

    tile = 512

    @pl.loop(0, out_ref.shape[1] // tile)
    def _(n):
        at = pl.ds(pl.multiple_of(n * tile, tile), tile)
        out_ref[:, at] = dot(x_ref[...], weight_ref[:, at])


def last(facts, x3, x2a, x2b, parts, weight):
    rows, depth = x3.shape
    width = weight.shape[1]
    return pl.pallas_call(
        last_kernel,
        out_shape=[
            jax.ShapeDtypeStruct((2 * rows, width), F32),
            jax.ShapeDtypeStruct((len(parts) * parts[0].shape[0], width), parts[0].dtype),
        ],
        in_specs=[SMEM] + [VMEM] * (4 + len(parts)),
        out_specs=[VMEM, VMEM],
        scratch_shapes=[pltpu.VMEM((2 * rows, depth), weight.dtype)],
        compiler_params=pltpu.CompilerParams(vmem_limit_bytes=LAST_LIMIT),
        cost_estimate=cost(2 * rows, weight),
    )(facts, x3, x2a, x2b, *parts, weight)


def dot(a, b):
    return jnp.dot(a, b, preferred_element_type=F32)


def gray(v):
    return v ^ (v >> 1)


def line_of_four(tokens, token_adapter_index, query_weight, shrink_weight, expand_weight):
    me = lax.axis_index("adapter")
    tp = lax.axis_index("tp")
    planes = [me] + [gray((gray(me) + i) % 4) for i in range(1, 4)]
    own = tokens[0]
    rows = own.shape[0]
    half = rows // 2
    width = query_weight.shape[1]
    shrink = shrink_weight[0]
    rank = shrink.shape[1]
    ids = token_adapter_index[0]

    x1 = shift(own, FROM_NEXT)
    inner = (me == 1) | (me == 2)
    base0 = stream(own, query_weight, FIRST_LIMIT)
    own, base0 = lax.optimization_barrier((own, base0))
    x3 = shift(own, FROM_LAST)

    inside = ("replica", "tp")
    peers = lax.axis_size(inside)
    peer = lax.axis_index(inside)
    group = lax.axis_index("groups")
    share = rank // peers // 2
    part = lax.dynamic_slice_in_dim(after(expand_weight[0], base0), (peer * 2 + group) * share, share)

    def columns(i):
        return lax.dynamic_slice_in_dim(part, planes[i] * width, width, 1)

    part = jnp.stack(
        [columns(0), shift(columns(3), FROM_NEXT), shift(columns(2), OPPOSITE), shift(columns(1), FROM_LAST)]
    )
    x1, part, own = lax.optimization_barrier((x1, part, own))
    x2a = shift(own, INNER)
    x2b = shift(x1, RELAY)
    part = jnp.concatenate([part.reshape(4 * share, width), swap(part, "groups").reshape(4 * share, width)])
    base1 = stream(after(x1, part), query_weight, NEXT_LIMIT)
    parts = [part] + [shift(part, [(i, i ^ k) for i in range(peers)], inside) for k in range(1, peers)]
    x3, x2a, x2b, base1 = lax.optimization_barrier((x3, x2a, x2b, base1))

    x2 = jnp.where(inner, x2a, x2b)
    ranks = []
    for i, x in enumerate((own, x1, x2, x3)):
        named = lax.dynamic_slice_in_dim(ids, planes[i] * rows, rows) == me
        ranks.append(jnp.where(named, dot(x, shrink), 0.0).astype(BF16))
    ranks = jnp.concatenate(ranks)
    ranks = [ranks, shift(ranks, FROM_NEXT), shift(ranks, OPPOSITE), shift(ranks, FROM_LAST)]
    facts = jnp.stack([inner.astype(jnp.int32), peer.astype(jnp.int32), group.astype(jnp.int32)])
    base23, panels = last(facts, x3, x2a, x2b, parts, query_weight)
    base = [base0, base1, base23[:rows], base23[rows:]]

    def rank_at(j, k):
        return ranks[j][k * rows:][:rows]

    wide = [jnp.concatenate([rank_at(j, (i - j) % 4) for j in range(4)], 1) for i in range(4)]

    def partial(side):
        at = side * half
        take = lambda x: lax.dynamic_slice_in_dim(x, at, half)
        ranks = jnp.concatenate([take(x) for x in wide])
        bases = jnp.concatenate([take(x) for x in base])
        return bases + LOW_RANK_SCALE * dot(ranks, panels)

    theirs = swap(partial(1 - tp).astype(BF16), "tp")
    full = (partial(tp) + theirs).astype(BF16).reshape(4, half, width)
    back = [full[0], shift(full[3], FROM_NEXT), shift(full[2], OPPOSITE), shift(full[1], FROM_LAST)]
    return place(jnp.stack(planes).astype(jnp.int32), back)[None]


def any_length(tokens, token_adapter_index, query_weight, shrink_weight, expand_weight):
    own_rows = tokens[0]
    tok_rows = own_rows.shape[0]
    features = own_rows.shape[1]
    neighbor_count = lax.axis_size("adapter")
    slot_capacity = max(2, 2 * tok_rows // neighbor_count)
    own_index = lax.axis_index("adapter")
    tp_index = lax.axis_index("tp")
    all_ids = token_adapter_index[0, :, 0]
    by_source = all_ids.reshape(neighbor_count, tok_rows)
    matches = (
        by_source[:, :, None] == jnp.arange(neighbor_count, dtype=jnp.int32)[None, None, :]
    ).astype(jnp.int32)
    order_in = jnp.sum((jnp.cumsum(matches, axis=1) - matches) * matches, axis=2)
    slot_index = by_source * slot_capacity + order_in
    send_slots = lax.dynamic_index_in_dim(slot_index, own_index, 0, keepdims=False)
    slot_range = jnp.arange(neighbor_count * slot_capacity, dtype=jnp.int32)
    partial_value = jnp.dot(
        lax.all_gather(own_rows, "adapter", axis=0, tiled=True),
        query_weight,
        preferred_element_type=jnp.float32,
    )
    packer = (slot_range[:, None] == send_slots[None, :]).astype(jnp.bfloat16)
    outgoing = jnp.dot(packer, own_rows, preferred_element_type=jnp.float32).astype(jnp.bfloat16)
    outgoing = outgoing.reshape(neighbor_count, slot_capacity, features)
    received_rows = lax.all_to_all(
        outgoing, "adapter", split_axis=0, concat_axis=0, tiled=True
    ).reshape(neighbor_count * slot_capacity, features)
    shrink_output = jnp.dot(received_rows, shrink_weight[0], preferred_element_type=jnp.float32)
    rank_activation = lax.psum(shrink_output, "tp").astype(jnp.bfloat16)
    half_rows = tok_rows // 2
    low_rank_delta = (
        LOW_RANK_SCALE
        * jnp.dot(rank_activation, expand_weight[0], preferred_element_type=jnp.float32)
    ).astype(jnp.bfloat16)
    returned = lax.all_to_all(
        low_rank_delta.reshape(neighbor_count, slot_capacity, -1),
        "adapter",
        split_axis=0,
        concat_axis=0,
        tiled=True,
    )
    returned = returned.reshape(neighbor_count * slot_capacity, -1)
    my_slots = lax.dynamic_slice_in_dim(send_slots, tp_index * half_rows, half_rows)
    placer = (my_slots[:, None] == slot_range[None, :]).astype(jnp.bfloat16)
    added = jnp.dot(placer, returned, preferred_element_type=jnp.float32)
    moved = lax.all_to_all(partial_value, "adapter", split_axis=0, concat_axis=1, tiled=True)
    home_rows = lax.psum_scatter(moved, "tp", scatter_dimension=0, tiled=True)
    queries = (home_rows + added).astype(jnp.bfloat16)
    return queries[None]


def solution(mesh):
    placed = (
        P(("groups", "replica"), "adapter", "tp"),
        P(("groups", "replica"), None, None),
        P("tp", "adapter"),
        P("adapter", "tp", None),
        P("adapter", None, None),
    )
    four = mesh.shape["adapter"] == 4 and all(mesh.shape[a] == 2 for a in ("groups", "replica", "tp"))
    return jax.shard_map(
        line_of_four if four else any_length,
        mesh=mesh,
        in_specs=placed,
        out_specs=P(("groups", "replica"), ("adapter", "tp"), None),
        check_vma=False,
    )
```
